256 devices in a mesh: row: 16 (over z, x_hi), col: 16 (over x_lo, y, core).
Axes of the slice: x: 4 (x_hi: 2, x_lo: 2; x = x_hi * 2 + x_lo), y: 4, z: 8, core: 2. Of those that a mesh axis runs over, the one named last changes fastest.
Arguments:
- blocks: bfloat16 [16, 16, 16, 64, 1024], P('row', 'col'), may hold values from -6 to 6
- order: int32 [16, 16, 16], P('row', 'col'), may hold values from 0 to 15, each once within a row
- cross_weights: bfloat16 [6, 16, 16, 8, 128, 128], P(None, 'row', 'col'), may hold values from -0.5 to 0.5
- local_weights: bfloat16 [12, 16, 16, 8, 128, 128], P(None, 'row', 'col'), may hold values from -0.5 to 0.5
Outputs:
- result: bfloat16 [16, 16, 16, 64, 1024], P('row', 'col')
The draws below stay inside these ranges and needn't reach their ends.
Inputs may be any that keep to these rules, and one draw needn't show every extreme that they name: Each rank's row of order is a permutation of 0 to 15.
All inputs are finite; a program needn't handle non-finite values.
Results may differ from the reference program's by a relative error of at most 0.033.
Values may be sent and summed in bfloat16 or wider, within the bound.
No kernel may reach another device: no remote copies, remote signals or barrier semaphores. Data moves between devices by JAX's collectives and lax.ppermute only.
A program may use at most 64 MiB of HBM per device.

```python
import jax
import jax.numpy as jnp

R = 64
S = 1024
BLK = 16
SECTIONS = 3
LOCAL = 4
HALF = 8
CROSS = 6
LOCALS = 12
N_ROW = 16
N_COL = 16


def block_scale(stream_key, shape, split, least, high):
    gain, own = 1.0, jax.random.fold_in(stream_key, 6)
    for position, parts in split:
        heights = jnp.exp(jax.random.uniform(jax.random.fold_in(own, position), (parts,), jnp.float32, least / len(split), high / len(split)))
        gain = gain * jnp.repeat(heights, shape[position] // parts).reshape([-1 if axis == position else 1 for axis in range(len(shape))])
    return gain


def scatter_about(rng, extent, scale, limit, pieces=(), held_as=jnp.bfloat16):
    entries = jax.random.normal(rng, extent, jnp.float32) * scale
    if len(pieces) > 0:
        entries = block_scale(rng, extent, pieces, -0.22, 0.18) * entries
    return jnp.clip(entries, min=-limit, max=limit).astype(held_as)


def setup_inputs(seed: int = 0) -> dict:
    arg_keys = jax.random.split(jax.random.key(seed), 5)
    return {
        "blocks": scatter_about(arg_keys[0], (N_ROW, N_COL, BLK, R, S), 1.0, 6.0, ((0, 16), (1, 16))),
        "order": jax.vmap(lambda own: jax.random.permutation(own, BLK))(jax.random.split(arg_keys[1], N_ROW * N_COL)).reshape((N_ROW, N_COL, BLK)).astype(jnp.int32),
        "cross_weights": scatter_about(arg_keys[2], (CROSS, N_ROW, N_COL, HALF, 2 * R, 2 * R), (2 * R) ** -0.5, 0.5, ((1, 16), (2, 16))),
        "local_weights": scatter_about(arg_keys[3], (LOCALS, N_ROW, N_COL, HALF, 2 * R, 2 * R), (2 * R) ** -0.5, 0.5, ((1, 16), (2, 16))),
    }


def pair_apply(weight, stacked):
    product = jnp.einsum("abhij,abhjs->abhis", weight.astype(jnp.float32), stacked.astype(jnp.float32))
    shape = product.shape
    return product.reshape(shape[0], shape[1], shape[2] * 2, shape[3] // 2, shape[4]).astype(jnp.bfloat16)


def cross_level(coeffs, weight, axis_pos, bit_pos, count):
    positions = jnp.arange(count, dtype=jnp.int32)
    partner = jnp.bitwise_xor(positions, jnp.int32(1 << bit_pos))
    upper_side = ((positions >> bit_pos) & 1) == 1
    shape = [1, 1, 1, 1, 1]
    shape[axis_pos] = count
    upper_side = upper_side.reshape(shape)
    mirrored = jnp.take(coeffs, partner, axis=axis_pos)
    half_count = coeffs.shape[2] // 2
    lower, upper = coeffs[:, :, :half_count], coeffs[:, :, half_count:]
    lower_far, upper_far = mirrored[:, :, :half_count], mirrored[:, :, half_count:]
    top = jnp.where(upper_side, upper_far, lower)
    bottom = jnp.where(upper_side, upper, lower_far)
    return pair_apply(weight, jnp.concatenate([top, bottom], axis=3))


def local_level(coeffs, weight):
    half_count = coeffs.shape[2] // 2
    stacked = jnp.concatenate([coeffs[:, :, :half_count], coeffs[:, :, half_count:]], axis=3)
    return pair_apply(weight, stacked)


def reference(blocks, order, cross_weights, local_weights):
    coeffs = jax.vmap(jax.vmap(lambda source, picks: source[picks]))(blocks, order)
    row_bits = N_ROW.bit_length() - 1
    col_bits = N_COL.bit_length() - 1
    for section_index in range(SECTIONS):
        coeffs = cross_level(coeffs, cross_weights[2 * section_index], 0, section_index % row_bits, N_ROW)
        coeffs = cross_level(coeffs, cross_weights[2 * section_index + 1], 1, section_index % col_bits, N_COL)
        for level_index in range(LOCAL):
            coeffs = local_level(coeffs, local_weights[section_index * LOCAL + level_index])
    return coeffs
```

```python
import functools

import jax
import jax.numpy as jnp
from jax import lax
from jax.experimental import pallas as pl
from jax.experimental.pallas import tpu as pltpu
from jax.sharding import PartitionSpec as P

SECTIONS = 3
LOCAL = 4
SIZES = (256, 256, 256, 256)
ORDER = (0, 1, 0, 3, 1, 0, 2, 3, 1, 0, 2, 3, 1, 0, 2, 3, 1, 2, 3, 1, 0, 2, 3, 2)
LIMIT = 8 * 2**20

VM = pl.BlockSpec(memory_space=pltpu.VMEM)
ANY = pl.BlockSpec(memory_space=pl.ANY)


def in_vmem(shape):
    return pltpu.VMEM(shape, jnp.bfloat16)


def held(x):
    return pltpu.with_memory_space_constraint(x, pltpu.VMEM)


def outside(x):
    return pltpu.with_memory_space_constraint(x, pltpu.HBM)


def swapped(piece, axis, bit):
    return lax.ppermute(piece, axis, [(i, i ^ 1 << bit) for i in range(lax.axis_size(axis))])


def side(level):
    return lax.axis_index(("row", "col")[level % 2]) >> (level // 2) & 1


def call(kernel, name, out_shape, in_specs, out_specs, scratch=(), aliases=None):
    return pl.pallas_call(
        kernel,
        out_shape=out_shape,
        in_specs=in_specs,
        out_specs=out_specs,
        scratch_shapes=list(scratch),
        input_output_aliases=aliases or {},
        compiler_params=pltpu.CompilerParams(vmem_limit_bytes=LIMIT),
        cost_estimate=pl.CostEstimate(flops=1, bytes_accessed=1, transcendentals=0),
        name=name,
    )


def picked(source, order, first, start, columns, out):
    for j in range(8):
        out[j] = source[order[0, first + j], :, start : start + columns]


def first_kernel(columns, order_any, blocks, held_blocks, keep, send, order, sems):
    index = pltpu.make_async_copy(order_any, order, sems.at[0])
    index.start()
    copies = [
        pltpu.make_async_copy(blocks.at[pl.ds(2 * j, 2)], held_blocks.at[pl.ds(2 * j, 2)], sems.at[1 + j])
        for j in range(8)
    ]
    for copy in copies:
        copy.start()
    index.wait()
    for copy in copies:
        copy.wait()
    upper = side(0)
    picked(held_blocks, order, 8 - 8 * upper, 0, columns, send)
    picked(held_blocks, order, 8 * upper, 0, columns, keep)


def first_take(order, blocks, columns):
    half = in_vmem((8, 64, columns))
    return call(
        functools.partial(first_kernel, columns),
        "take_first",
        (in_vmem(blocks.shape), half, half),
        [ANY, ANY],
        (VM, VM, VM),
        [pltpu.SMEM((1, 16), jnp.int32), pltpu.SemaphoreType.DMA((9,))],
    )(outside(order[None]), outside(blocks))


def later_kernel(starts, sizes, order_any, blocks, token, *refs):
    outs, order, sem = refs[:-2], refs[-2], refs[-1]
    index = pltpu.make_async_copy(order_any, order, sem)
    index.start()
    index.wait()
    upper = side(0)
    for c, (start, columns) in enumerate(zip(starts, sizes)):
        picked(blocks, order, 8 - 8 * upper, start, columns, outs[2 * c + 1])
        picked(blocks, order, 8 * upper, start, columns, outs[2 * c])


def later_takes(order, blocks, token, starts, sizes):
    halves = [in_vmem((8, 64, n)) for n in sizes for _ in range(2)]
    outs = call(
        functools.partial(later_kernel, starts, sizes),
        "take_later",
        tuple(halves),
        [ANY, VM, ANY],
        (VM,) * len(halves),
        [pltpu.SMEM((1, 16), jnp.int32), pltpu.SemaphoreType.DMA],
    )(outside(order[None]), held(blocks), token)
    return list(zip(outs[::2], outs[1::2]))


def crossed(keep, arrived, weight, upper, h):
    own, other = keep[h], arrived[h]
    top = jnp.where(upper == 1, other, own)
    bottom = jnp.where(upper == 1, own, other)
    stacked = jnp.concatenate([top, bottom], axis=0)
    product = jnp.dot(weight[h], stacked, preferred_element_type=jnp.float32)
    return product.astype(jnp.bfloat16).reshape(2, 64, stacked.shape[1])


def row_kernel(level, keep, arrived, cross, token, keep_out, send_out):
    upper, later = side(level), side(level + 1)
    weight = cross.at[level]
    for p in range(4):
        send_out[2 * p : 2 * p + 2] = crossed(keep, arrived, weight, upper, 4 - 4 * later + p)
    for p in range(4):
        keep_out[2 * p : 2 * p + 2] = crossed(keep, arrived, weight, upper, 4 * later + p)


def row_level(level, keep, arrived, cross, token):
    half = in_vmem(keep.shape)
    return call(
        functools.partial(row_kernel, level),
        f"row_{level}",
        (half, half),
        [VM, VM, VM, ANY],
        (VM, VM),
    )(held(keep), held(arrived), cross, token)


def combined(first, second, upper, out):
    for j in range(4):
        halves = []
        for g in (j, 4 + j):
            weight = first[g]
            if upper is not None:
                turned = jnp.concatenate([weight[:, 64:], weight[:, :64]], axis=1)
                weight = jnp.where(upper == 1, turned, weight)
            halves.append(weight)
        for t in range(2):
            for i in range(2):
                out[j, 128 * t : 128 * t + 128, 128 * i : 128 * i + 128] = jnp.dot(
                    second[2 * j + t][:, 64 * i : 64 * i + 64],
                    halves[i][64 * t : 64 * t + 64],
                    preferred_element_type=jnp.float32,
                ).astype(jnp.bfloat16)


def combine_kernel(cross, local, token, *outs):
    for section in range(SECTIONS):
        level, k = 2 * section + 1, section * LOCAL
        combined(cross.at[level], local.at[k], side(level), outs[2 * section])
        combined(local.at[k + 1], local.at[k + 2], None, outs[2 * section + 1])


def combine(cross, local, token):
    return call(
        combine_kernel,
        "combine",
        (in_vmem((4, 256, 256)),) * (2 * SECTIONS),
        [VM, VM, ANY],
        (VM,) * (2 * SECTIONS),
    )(cross, local, token)


def four(weight, blocks):
    stacked = jnp.concatenate(blocks, axis=0)
    product = jnp.dot(weight, stacked, preferred_element_type=jnp.float32)
    return product.astype(jnp.bfloat16).reshape(4, 64, stacked.shape[1])


def mixed(buf, source, weight, h):
    stacked = jnp.concatenate([buf[source, h], buf[source, 8 + h]], axis=0)
    product = jnp.dot(weight, stacked, preferred_element_type=jnp.float32)
    return product.astype(jnp.bfloat16).reshape(2, 64, stacked.shape[1])


def col_levels(keep, arrived, early, late, buf):
    for j in range(4):
        buf[0, 4 * j : 4 * j + 4] = four(
            early[j], [keep[j], arrived[j], keep[4 + j], arrived[4 + j]]
        )
    for j in range(4):
        buf[1, 4 * j : 4 * j + 4] = four(
            late[j], [buf[0, j], buf[0, 8 + j], buf[0, 4 + j], buf[0, 12 + j]]
        )


def col_kernel(level, keep, arrived, early, late, local, token, keep_out, send_out, buf):
    col_levels(keep, arrived, early, late, buf)
    last, later = level // 2 * LOCAL + LOCAL - 1, side(level + 1)
    for first, out in ((4 - 4 * later, send_out), (4 * later, keep_out)):
        for p in range(4):
            out[2 * p : 2 * p + 2] = mixed(buf, 1, local[last, first + p], first + p)


def col_level(level, keep, arrived, weights, token):
    half = in_vmem(keep.shape)
    return call(
        functools.partial(col_kernel, level),
        f"col_{level}",
        (half, half),
        [VM, VM, VM, VM, VM, ANY],
        (VM, VM),
        [pltpu.VMEM((2, 16, 64, keep.shape[2]), jnp.bfloat16)],
    )(held(keep), held(arrived), *weights, token)


def last_kernel(level, start, columns, *refs):
    keep, arrived, early, late, local = refs[:5]
    out, buf, done, sems = refs[-4:]
    col_levels(keep, arrived, early, late, buf)
    last = level // 2 * LOCAL + LOCAL - 1
    copies = []
    for h in range(8):
        done[2 * h : 2 * h + 2] = mixed(buf, 1, local[last, h], h)
        copy = pltpu.make_async_copy(
            done.at[pl.ds(2 * h, 2)],
            out.at[pl.ds(2 * h, 2), :, pl.ds(start, columns)],
            sems.at[h],
        )
        copy.start()
        copies.append(copy)
    for copy in copies:
        copy.wait()


def last_level(level, keep, arrived, weights, token, result, start, total):
    columns = keep.shape[2]
    operands = [held(keep), held(arrived), *weights]
    in_specs = [VM] * 5
    aliases = {}
    if result is not None:
        operands.append(outside(result))
        in_specs.append(ANY)
        aliases = {5: 0}
    if token is not None:
        operands.append(token)
        in_specs.append(ANY)
    return call(
        functools.partial(last_kernel, level, start, columns),
        f"last_{start}",
        pltpu.HBM((16, 64, total), jnp.bfloat16),
        in_specs,
        ANY,
        [
            pltpu.VMEM((2, 16, 64, columns), jnp.bfloat16),
            pltpu.VMEM((16, 64, columns), jnp.bfloat16),
            pltpu.SemaphoreType.DMA((8,)),
        ],
        aliases,
    )(*operands)


def shards(blocks, order, cross_weights, local_weights):
    blocks, order = blocks[0, 0], order[0, 0]
    cross, local = held(cross_weights[:, 0, 0]), held(local_weights[:, 0, 0])
    total = blocks.shape[2]
    starts = [sum(SIZES[:c]) for c in range(len(SIZES))]
    result = None
    blocks, keep, send = first_take(order, blocks, SIZES[0])
    state = [(keep, swapped(send, "row", 0))]
    for token, send in later_takes(order, blocks, keep, starts[1:], SIZES[1:]):
        state.append((token, swapped(send, "row", 0)))
    pairs = combine(cross, local, token)
    token, stages = pairs[0], [0] * len(SIZES)
    ended = False
    for c in ORDER:
        stages[c] += 1
        stage, level = stages[c], stages[c] - 1
        keep, arrived = state[c]
        weights = (*(held(pair) for pair in pairs[level // 2 * 2 : level // 2 * 2 + 2]), local)
        if level == 2 * SECTIONS - 1:
            result = last_level(
                level, keep, arrived, weights, None if ended else token, result, starts[c], total
            )
            token, ended = outside(result), True
            continue
        ended = False
        if level % 2 == 0:
            keep, send = row_level(level, keep, arrived, cross, token)
        else:
            keep, send = col_level(level, keep, arrived, weights, token)
        state[c] = keep, swapped(send, ("row", "col")[stage % 2], stage // 2)
        token = keep
    return result[None, None]


def solution(mesh):
    placed = (
        P("row", "col", None, None, None),
        P("row", "col", None),
        P(None, "row", "col", None, None, None),
        P(None, "row", "col", None, None, None),
    )
    return jax.shard_map(
        shards,
        mesh=mesh,
        in_specs=placed,
        out_specs=P("row", "col", None, None, None),
        check_vma=False,
    )
```

```python
import jax
import jax.numpy as jnp
from jax import lax
from jax.experimental import pallas as pl
from jax.experimental.pallas import tpu as pltpu
from jax.sharding import PartitionSpec as P

SECTIONS = 3
LOCAL = 4
SIZES = (256, 256, 256, 256)
FLOWS = ("rrc", "rcc", "rcr", "rpp")
LATER, COMBINE = -1, -2
ORDER = (0, LATER, 3, COMBINE, 1, 2, 0, 1, 0, 2, 1, 3, 2, 1, 0, 2, 1, 2, 0, 1, 3, 2, 0, 3)
LIMIT = 10 * 2**20

VM = pl.BlockSpec(memory_space=pltpu.VMEM)
ANY = pl.BlockSpec(memory_space=pl.ANY)


def in_vmem(*shape):
    return pltpu.VMEM(shape, jnp.bfloat16)


def held(x):
    return pltpu.with_memory_space_constraint(x, pltpu.VMEM)


def outside(x):
    return pltpu.with_memory_space_constraint(x, pltpu.HBM)


def row_side(section):
    return lax.axis_index("row") >> section & 1


def col_side(section):
    return lax.axis_index("col") >> section & 1


def swapped(piece, axis, section):
    size = lax.axis_size(axis)
    return lax.ppermute(piece, axis, [(i, i ^ 1 << section) for i in range(size)])


def swapped_both(piece, section):
    rows, cols, bit = lax.axis_size("row"), lax.axis_size("col"), 1 << section
    pairs = [(i * cols + j, (i ^ bit) * cols + (j ^ bit)) for i in range(rows) for j in range(cols)]
    return lax.ppermute(piece, ("row", "col"), pairs)


def call(kernel, name, out_shape, operands, token, out_specs=None, scratch=(), result=None):
    operands, specs = list(operands), [ANY if memory == "any" else VM for _, memory in operands]
    operands = [outside(x) if memory == "any" else held(x) for x, memory in operands]
    aliases = {}
    if result is not None:
        aliases = {len(operands): 0}
        operands.append(outside(result))
        specs.append(ANY)
    if token is not None:
        operands.append(token)
        specs.append(ANY)
    extra = len(operands)

    def body(*refs):
        kernel(refs[:extra], refs[extra : extra + len(out_shape)], refs[extra + len(out_shape) :])

    return pl.pallas_call(
        body,
        out_shape=tuple(out_shape),
        in_specs=specs,
        out_specs=(VM,) * len(out_shape) if out_specs is None else out_specs,
        scratch_shapes=list(scratch),
        input_output_aliases=aliases,
        compiler_params=pltpu.CompilerParams(vmem_limit_bytes=LIMIT),
        cost_estimate=pl.CostEstimate(flops=1, bytes_accessed=1, transcendentals=0),
        name=name,
    )(*operands)


def vmem(*arrays):
    return [(x, "vmem") for x in arrays]


def pieces(flow, section):
    row, col = row_side(section), col_side(section)
    if flow == "c":
        return [[(8 * row, 8)], [(8 - 8 * row, 8)]]
    own, by_col, by_row, by_both = [(8 * r + 4 * c, 4) for r in (row, 1 - row) for c in (col, 1 - col)]
    if flow == "p":
        return [[own], [by_row], [by_col], [by_both]]
    return [[own], [by_row], [by_col, by_both]]


COUNTS = {"c": (8, 8), "p": (4, 4, 4, 4), "r": (4, 4, 8)}


def shapes(flow, columns):
    return [in_vmem(count, 64, columns) for count in COUNTS[flow]]


def sent(flow, section, outs):
    if flow == "c":
        return outs[0], swapped(outs[1], "row", section)
    if flow == "p":
        return (
            outs[0],
            swapped(outs[1], "row", section),
            swapped(outs[2], "col", section),
            swapped_both(outs[3], section),
        )
    return outs[0], outs[1], swapped(outs[2], "col", section)


def picked(source, order, start, columns, outs):
    for ranges, out in zip(pieces("r", 0), outs):
        at = 0
        for first, count in ranges:
            for j in range(count):
                out[at] = source[order[0, first + j], :, start : start + columns]
                at += 1


def first_take(order, blocks, columns):
    def kernel(ins, outs, scratch):
        (order_any, source), (order_held, sems) = ins, scratch
        index = pltpu.make_async_copy(order_any, order_held, sems.at[0])
        whole = pltpu.make_async_copy(source, outs[0], sems.at[1])
        whole.start()
        index.start()
        index.wait()
        whole.wait()
        picked(outs[0], order_held, 0, columns, outs[1:])

    return call(
        kernel,
        "take_first",
        [in_vmem(*blocks.shape), *shapes("r", columns)],
        [(order, "any"), (blocks, "any")],
        None,
        scratch=[pltpu.SMEM((1, 16), jnp.int32), pltpu.SemaphoreType.DMA((2,))],
    )


def later_takes(order, blocks, cross, starts, sizes, token):
    total = sum(sizes)

    def kernel(ins, outs, scratch):
        (order_any, source, weights, _), (order_held, sem) = ins, scratch
        index = pltpu.make_async_copy(order_any, order_held, sem)
        index.start()
        for section in range(SECTIONS):
            for p in range(4):
                outs[section][p] = weights[2 * section, 4 - 4 * col_side(section) + p]
        index.wait()
        together = outs[SECTIONS]
        for c, (start, columns) in enumerate(zip(starts, sizes)):
            at = start - starts[0]
            own, by_row = outs[SECTIONS + 1 + 2 * c : SECTIONS + 3 + 2 * c]
            part = together.at[:, :, at : at + columns]
            picked(source, order_held, start, columns, (own, by_row, part))

    outs = call(
        kernel,
        "take_later",
        [in_vmem(4, 128, 128)] * SECTIONS
        + [in_vmem(8, 64, total)]
        + [in_vmem(4, 64, n) for n in sizes for _ in range(2)],
        [(order, "any"), *vmem(blocks, cross)],
        token,
        scratch=[pltpu.SMEM((1, 16), jnp.int32), pltpu.SemaphoreType.DMA],
    )
    return outs[:SECTIONS], outs[SECTIONS], list(zip(outs[SECTIONS + 1 :: 2], outs[SECTIONS + 2 :: 2]))


def combined(first, second, upper, out):
    for j in range(4):
        halves = []
        for g in (j, 4 + j):
            weight = first[g]
            if upper is not None:
                turned = jnp.concatenate([weight[:, 64:], weight[:, :64]], axis=1)
                weight = jnp.where(upper == 1, turned, weight)
            halves.append(weight)
        for t in range(2):
            for i in range(2):
                out[j, 128 * t : 128 * t + 128, 128 * i : 128 * i + 128] = jnp.dot(
                    second[2 * j + t][:, 64 * i : 64 * i + 64],
                    halves[i][64 * t : 64 * t + 64],
                    preferred_element_type=jnp.float32,
                ).astype(jnp.bfloat16)


def combine(cross, local, token):
    def kernel(ins, outs, scratch):
        cross, local = ins[:2]
        for section in range(SECTIONS):
            level, k = 2 * section + 1, section * LOCAL
            combined(cross.at[level], local.at[k], col_side(section), outs[2 * section])
            combined(local.at[k + 1], local.at[k + 2], None, outs[2 * section + 1])

    return call(kernel, "combine", [in_vmem(4, 256, 256)] * (2 * SECTIONS), vmem(cross, local), token)


def times(weight, blocks):
    stacked = jnp.concatenate(blocks, axis=0)
    product = jnp.dot(weight, stacked, preferred_element_type=jnp.float32)
    return product.astype(jnp.bfloat16).reshape(len(blocks), 64, stacked.shape[1])


def paired(weight, upper, own, other):
    return times(weight, [jnp.where(upper == 1, other, own), jnp.where(upper == 1, own, other)])


def row_step(section, keep, arrived, cross, token):
    def kernel(ins, outs, scratch):
        keep, arrived, cross = ins[:3]
        row, col = row_side(section), col_side(section)
        for first, out in ((4 - 4 * col, outs[1]), (4 * col, outs[0])):
            for p in range(4):
                h = first + p
                out[2 * p : 2 * p + 2] = paired(cross[2 * section, h], row, keep[h], arrived[h])

    shape = in_vmem(*keep.shape)
    return call(kernel, f"row_{section}", [shape, shape], vmem(keep, arrived, cross), token)


def relay_step(section, by_row, arrived, offset, token):
    columns = by_row.shape[2]

    def kernel(ins, outs, scratch):
        outs[0][:4] = ins[0][...]
        outs[0][4:] = ins[1][4:, :, offset : offset + columns]

    return call(kernel, f"relay_{section}", [in_vmem(8, 64, columns)], vmem(by_row, arrived), token)


def end_step(section, flow, after, state, weights, token, result, start, total):
    early, late, local, cross, lent = weights
    columns = state[0].shape[2]
    pieces_in, offset = state, 0
    if flow == "r":
        *pieces_in, offset = state
    operands = vmem(*pieces_in, early, late, local)
    if flow != "c":
        operands += vmem(cross, lent)
    n = len(pieces_in)

    def halves(ins, buf):
        if flow == "c":
            return (lambda j: ins[0][j]), (lambda j: ins[1][j])
        own, row, col = ins[0], row_side(section), col_side(section)
        if flow == "p":
            by_row, by_col, by_both = (lambda p: ins[1][p]), (lambda p: ins[2][p]), (lambda p: ins[3][p])
        else:
            by_col = lambda p: ins[1][p, :, offset : offset + columns]
            by_row, by_both = (lambda p: ins[2][p]), (lambda p: ins[2][4 + p])
        cross, lent = ins[n + 3], ins[n + 4]
        for p in range(4):
            buf[1, 2 * p : 2 * p + 2] = paired(cross[2 * section, 4 * col + p], row, own[p], by_row(p))
            buf[1, 8 + 2 * p : 10 + 2 * p] = paired(lent[p], row, by_col(p), by_both(p))
        return (lambda j: buf[1, j]), (lambda j: buf[1, 8 + j])

    def kernel(ins, outs, scratch):
        buf = scratch[0]
        early, late, local = ins[n : n + 3]
        mine, theirs = halves(ins, buf)
        for j in range(4):
            buf[0, 4 * j : 4 * j + 4] = times(early[j], [mine(j), theirs(j), mine(4 + j), theirs(4 + j)])
        for j in range(4):
            buf[1, 4 * j : 4 * j + 4] = times(late[j], [buf[0, j], buf[0, 8 + j], buf[0, 4 + j], buf[0, 12 + j]])
        last = section * LOCAL + LOCAL - 1

        def final(h):
            return times(local[last, h], [buf[1, h], buf[1, 8 + h]])

        if after is not None:
            for ranges, out in list(zip(pieces(after, section + 1), outs))[::-1]:
                at = 0
                for first, count in ranges:
                    for p in range(count // 2):
                        out[at : at + 2] = final(first // 2 + p)
                        at += 2
            return
        done, sems = scratch[1:]
        copies = []
        for h in range(8):
            done[2 * h : 2 * h + 2] = final(h)
            copy = pltpu.make_async_copy(
                done.at[pl.ds(2 * h, 2)],
                outs[0].at[pl.ds(2 * h, 2), :, pl.ds(start, columns)],
                sems.at[h],
            )
            copy.start()
            copies.append(copy)
        for copy in copies:
            copy.wait()

    scratch = [in_vmem(2, 16, 64, columns)]
    if after is not None:
        return call(
            kernel, f"end_{section}", shapes(after, columns), operands, token, scratch=scratch
        )
    scratch += [in_vmem(16, 64, columns), pltpu.SemaphoreType.DMA((8,))]
    return call(
        kernel,
        f"end_{section}",
        [pltpu.HBM((16, 64, total), jnp.bfloat16)],
        operands,
        token,
        out_specs=(ANY,),
        scratch=scratch,
        result=result,
    )


def shards(blocks, order, cross_weights, local_weights):
    blocks, order = blocks[0, 0], order[0]
    cross, local = cross_weights[:, 0, 0], local_weights[:, 0, 0]
    total = blocks.shape[2]
    starts = [sum(SIZES[:c]) for c in range(len(SIZES))]
    blocks, *outs = first_take(order, blocks, SIZES[0])
    states = {0: (*sent("r", 0, outs), 0)}
    token, result, ended = outs[0], None, False
    sections, halfway = [0] * len(SIZES), [False] * len(SIZES)
    for c in ORDER:
        if c == LATER:
            lend, together, rest = later_takes(order, blocks, cross, starts[1:], SIZES[1:], token)
            arrived = swapped(together, "col", 0)
            for k, pair in enumerate(rest, 1):
                states[k] = (*pair, arrived, starts[k] - starts[1])
            lent = [
                swapped(lend[s], "col", s) if any(flows[s] != "c" for flows in FLOWS) else None
                for s in range(SECTIONS)
            ]
            token = together
            continue
        if c == COMBINE:
            pairs = combine(cross, local, token)
            token = pairs[0]
            continue
        section, state = sections[c], states[c]
        flow = FLOWS[c][section]
        if flow != "p" and not halfway[c]:
            halfway[c] = True
            if flow == "c":
                keep, send = row_step(section, *state, cross, token)
                states[c] = keep, swapped(send, "col", section)
                token = keep
            else:
                own, by_row, by_col, offset = state
                (joined,) = relay_step(section, by_row, by_col, offset, token)
                states[c] = own, by_col, swapped(joined, "row", section), offset
                token = joined
            ended = False
            continue
        weights = (*pairs[2 * section : 2 * section + 2], local, cross, lent[section])
        after = FLOWS[c][section + 1] if section < SECTIONS - 1 else None
        onto = result if after is None else None
        before = None if ended and onto is not None else token
        outs = end_step(section, flow, after, state, weights, before, onto, starts[c], total)
        sections[c], halfway[c] = section + 1, False
        if after is None:
            (result,) = outs
            token, ended = outside(result), True
        else:
            state = sent(after, section + 1, outs)
            states[c] = (*state, 0) if after == "r" else state
            token, ended = outs[0], False
    return result[None, None]


def solution(mesh):
    placed = (
        P("row", "col", None, None, None),
        P("row", "col", None),
        P(None, "row", "col", None, None, None),
        P(None, "row", "col", None, None, None),
    )
    return jax.shard_map(
        shards,
        mesh=mesh,
        in_specs=placed,
        out_specs=P("row", "col", None, None, None),
        check_vma=False,
    )
```

```python
import jax
import jax.numpy as jnp
from jax import lax
from jax.experimental import pallas as pl
from jax.experimental.pallas import tpu as pltpu
from jax.sharding import PartitionSpec as P

SECTIONS = 3
LOCAL = 4
SIZES = (256, 256, 256, 256)
FLOWS = ("rcp", "rpc", "rpp", "rpp")
LATER, COMBINE = -1, -2
ORDER = (0, LATER, 2, COMBINE, 1, 0, 1, 0, 2, 3, 1, 3, 0, 2, 1, 0, 3, 2, 1, 3)
LIMIT = 10 * 2**20

VM = pl.BlockSpec(memory_space=pltpu.VMEM)
ANY = pl.BlockSpec(memory_space=pl.ANY)


def in_vmem(*shape):
    return pltpu.VMEM(shape, jnp.bfloat16)


def held(x):
    return pltpu.with_memory_space_constraint(x, pltpu.VMEM)


def outside(x):
    return pltpu.with_memory_space_constraint(x, pltpu.HBM)


def row_side(section):
    return lax.axis_index("row") >> section & 1


def col_side(section):
    return lax.axis_index("col") >> section & 1


def swapped(piece, axis, section):
    size = lax.axis_size(axis)
    return lax.ppermute(piece, axis, [(i, i ^ 1 << section) for i in range(size)])


def swapped_both(piece, section):
    rows, cols, bit = lax.axis_size("row"), lax.axis_size("col"), 1 << section
    pairs = [(i * cols + j, (i ^ bit) * cols + (j ^ bit)) for i in range(rows) for j in range(cols)]
    return lax.ppermute(piece, ("row", "col"), pairs)


def call(kernel, name, out_shape, operands, token, out_specs=None, scratch=(), result=None):
    operands, specs = list(operands), [ANY if memory == "any" else VM for _, memory in operands]
    operands = [outside(x) if memory == "any" else held(x) for x, memory in operands]
    aliases = {}
    if result is not None:
        aliases = {len(operands): 0}
        operands.append(outside(result))
        specs.append(ANY)
    if token is not None:
        operands.append(token)
        specs.append(ANY)
    extra = len(operands)

    def body(*refs):
        kernel(refs[:extra], refs[extra : extra + len(out_shape)], refs[extra + len(out_shape) :])

    return pl.pallas_call(
        body,
        out_shape=tuple(out_shape),
        in_specs=specs,
        out_specs=(VM,) * len(out_shape) if out_specs is None else out_specs,
        scratch_shapes=list(scratch),
        input_output_aliases=aliases,
        compiler_params=pltpu.CompilerParams(vmem_limit_bytes=LIMIT),
        cost_estimate=pl.CostEstimate(flops=1, bytes_accessed=1, transcendentals=0),
        name=name,
    )(*operands)


def vmem(*arrays):
    return [(x, "vmem") for x in arrays]


def pieces(flow, section):
    row, col = row_side(section), col_side(section)
    if flow == "c":
        return [[(8 * row, 8)], [(8 - 8 * row, 8)]]
    own, by_col, by_row, by_both = [(8 * r + 4 * c, 4) for r in (row, 1 - row) for c in (col, 1 - col)]
    if flow == "p":
        return [[own], [by_row], [by_col], [by_both]]
    return [[own], [by_row], [by_col, by_both]]


COUNTS = {"c": (8, 8), "p": (4, 4, 4, 4), "r": (4, 4, 8)}


def shapes(flow, columns):
    return [in_vmem(count, 64, columns) for count in COUNTS[flow]]


def sent(flow, section, outs):
    if flow == "c":
        return outs[0], swapped(outs[1], "row", section)
    if flow == "p":
        return (
            outs[0],
            swapped(outs[1], "row", section),
            swapped(outs[2], "col", section),
            swapped_both(outs[3], section),
        )
    return outs[0], outs[1], swapped(outs[2], "col", section)


def picked(source, order, start, columns, outs):
    for ranges, out in zip(pieces("r", 0), outs):
        at = 0
        for first, count in ranges:
            for j in range(count):
                out[at] = source[order[0, first + j], :, start : start + columns]
                at += 1


def first_take(order, blocks, columns):
    def kernel(ins, outs, scratch):
        (order_any, source), (order_held, sems) = ins, scratch
        index = pltpu.make_async_copy(order_any, order_held, sems.at[0])
        whole = pltpu.make_async_copy(source, outs[0], sems.at[1])
        whole.start()
        index.start()
        index.wait()
        whole.wait()
        picked(outs[0], order_held, 0, columns, outs[1:])

    return call(
        kernel,
        "take_first",
        [in_vmem(*blocks.shape), *shapes("r", columns)],
        [(order, "any"), (blocks, "any")],
        None,
        scratch=[pltpu.SMEM((1, 16), jnp.int32), pltpu.SemaphoreType.DMA((2,))],
    )


def later_takes(order, blocks, cross, starts, sizes, token):
    total = sum(sizes)

    def kernel(ins, outs, scratch):
        (order_any, source, weights, _), (order_held, sem) = ins, scratch
        index = pltpu.make_async_copy(order_any, order_held, sem)
        index.start()
        for section in range(SECTIONS):
            for p in range(4):
                outs[section][p] = weights[2 * section, 4 - 4 * col_side(section) + p]
        index.wait()
        together = outs[SECTIONS]
        for c, (start, columns) in enumerate(zip(starts, sizes)):
            at = start - starts[0]
            own, by_row = outs[SECTIONS + 1 + 2 * c : SECTIONS + 3 + 2 * c]
            part = together.at[:, :, at : at + columns]
            picked(source, order_held, start, columns, (own, by_row, part))

    outs = call(
        kernel,
        "take_later",
        [in_vmem(4, 128, 128)] * SECTIONS
        + [in_vmem(8, 64, total)]
        + [in_vmem(4, 64, n) for n in sizes for _ in range(2)],
        [(order, "any"), *vmem(blocks, cross)],
        token,
        scratch=[pltpu.SMEM((1, 16), jnp.int32), pltpu.SemaphoreType.DMA],
    )
    return outs[:SECTIONS], outs[SECTIONS], list(zip(outs[SECTIONS + 1 :: 2], outs[SECTIONS + 2 :: 2]))


def combined(first, second, upper, out):
    for j in range(4):
        halves = []
        for g in (j, 4 + j):
            weight = first[g]
            if upper is not None:
                turned = jnp.concatenate([weight[:, 64:], weight[:, :64]], axis=1)
                weight = jnp.where(upper == 1, turned, weight)
            halves.append(weight)
        for t in range(2):
            for i in range(2):
                out[j, 128 * t : 128 * t + 128, 128 * i : 128 * i + 128] = jnp.dot(
                    second[2 * j + t][:, 64 * i : 64 * i + 64],
                    halves[i][64 * t : 64 * t + 64],
                    preferred_element_type=jnp.float32,
                ).astype(jnp.bfloat16)


def combine(cross, local, token):
    def kernel(ins, outs, scratch):
        cross, local = ins[:2]
        for section in range(SECTIONS):
            level, k = 2 * section + 1, section * LOCAL
            combined(cross.at[level], local.at[k], col_side(section), outs[2 * section])
            combined(local.at[k + 1], local.at[k + 2], None, outs[2 * section + 1])

    return call(kernel, "combine", [in_vmem(4, 256, 256)] * (2 * SECTIONS), vmem(cross, local), token)


def times(weight, blocks):
    stacked = jnp.concatenate(blocks, axis=0)
    product = jnp.dot(weight, stacked, preferred_element_type=jnp.float32)
    return product.astype(jnp.bfloat16).reshape(len(blocks), 64, stacked.shape[1])


def paired(weight, upper, own, other):
    return times(weight, [jnp.where(upper == 1, other, own), jnp.where(upper == 1, own, other)])


def row_step(section, keep, arrived, cross, token):
    def kernel(ins, outs, scratch):
        keep, arrived, cross = ins[:3]
        row, col = row_side(section), col_side(section)
        for first, out in ((4 - 4 * col, outs[1]), (4 * col, outs[0])):
            for p in range(4):
                h = first + p
                out[2 * p : 2 * p + 2] = paired(cross[2 * section, h], row, keep[h], arrived[h])

    shape = in_vmem(*keep.shape)
    return call(kernel, f"row_{section}", [shape, shape], vmem(keep, arrived, cross), token)


def relay_step(section, by_row, arrived, offset, token):
    columns = by_row.shape[2]

    def kernel(ins, outs, scratch):
        outs[0][:4] = ins[0][...]
        outs[0][4:] = ins[1][4:, :, offset : offset + columns]

    return call(kernel, f"relay_{section}", [in_vmem(8, 64, columns)], vmem(by_row, arrived), token)


def end_step(section, flow, after, state, weights, token, result, start, total):
    early, late, local, cross, lent = weights
    columns = state[0].shape[2]
    pieces_in, offset = state, 0
    if flow == "r":
        *pieces_in, offset = state
    operands = vmem(*pieces_in, early, late, local)
    if flow != "c":
        operands += vmem(cross, lent)
    n = len(pieces_in)

    def halves(ins, buf):
        if flow == "c":
            return (lambda j: ins[0][j]), (lambda j: ins[1][j])
        own, row, col = ins[0], row_side(section), col_side(section)
        if flow == "p":
            by_row, by_col, by_both = (lambda p: ins[1][p]), (lambda p: ins[2][p]), (lambda p: ins[3][p])
        else:
            by_col = lambda p: ins[1][p, :, offset : offset + columns]
            by_row, by_both = (lambda p: ins[2][p]), (lambda p: ins[2][4 + p])
        cross, lent = ins[n + 3], ins[n + 4]
        for p in range(4):
            buf[1, 2 * p : 2 * p + 2] = paired(cross[2 * section, 4 * col + p], row, own[p], by_row(p))
            buf[1, 8 + 2 * p : 10 + 2 * p] = paired(lent[p], row, by_col(p), by_both(p))
        return (lambda j: buf[1, j]), (lambda j: buf[1, 8 + j])

    def kernel(ins, outs, scratch):
        buf = scratch[0]
        early, late, local = ins[n : n + 3]
        mine, theirs = halves(ins, buf)
        for j in range(4):
            buf[0, 4 * j : 4 * j + 4] = times(early[j], [mine(j), theirs(j), mine(4 + j), theirs(4 + j)])
        for j in range(4):
            buf[1, 4 * j : 4 * j + 4] = times(late[j], [buf[0, j], buf[0, 8 + j], buf[0, 4 + j], buf[0, 12 + j]])
        last = section * LOCAL + LOCAL - 1

        def final(h):
            return times(local[last, h], [buf[1, h], buf[1, 8 + h]])

        if after is not None:
            for ranges, out in list(zip(pieces(after, section + 1), outs))[::-1]:
                at = 0
                for first, count in ranges:
                    for p in range(count // 2):
                        out[at : at + 2] = final(first // 2 + p)
                        at += 2
            return
        done, sems = scratch[1:]
        copies = []
        for h in range(8):
            done[2 * h : 2 * h + 2] = final(h)
            copy = pltpu.make_async_copy(
                done.at[pl.ds(2 * h, 2)],
                outs[0].at[pl.ds(2 * h, 2), :, pl.ds(start, columns)],
                sems.at[h],
            )
            copy.start()
            copies.append(copy)
        for copy in copies:
            copy.wait()

    scratch = [in_vmem(2, 16, 64, columns)]
    if after is not None:
        return call(
            kernel, f"end_{section}", shapes(after, columns), operands, token, scratch=scratch
        )
    scratch += [in_vmem(16, 64, columns), pltpu.SemaphoreType.DMA((8,))]
    return call(
        kernel,
        f"end_{section}",
        [pltpu.HBM((16, 64, total), jnp.bfloat16)],
        operands,
        token,
        out_specs=(ANY,),
        scratch=scratch,
        result=result,
    )


def shards(blocks, order, cross_weights, local_weights):
    blocks, order = blocks[0, 0], order[0]
    cross, local = cross_weights[:, 0, 0], local_weights[:, 0, 0]
    total = blocks.shape[2]
    starts = [sum(SIZES[:c]) for c in range(len(SIZES))]
    blocks, *outs = first_take(order, blocks, SIZES[0])
    states = {0: (*sent("r", 0, outs), 0)}
    token, result, ended = outs[0], None, False
    sections, halfway = [0] * len(SIZES), [False] * len(SIZES)
    for c in ORDER:
        if c == LATER:
            lend, together, rest = later_takes(order, blocks, cross, starts[1:], SIZES[1:], token)
            arrived = swapped(together, "col", 0)
            for k, pair in enumerate(rest, 1):
                states[k] = (*pair, arrived, starts[k] - starts[1])
            lent = [
                swapped(lend[s], "col", s) if any(flows[s] != "c" for flows in FLOWS) else None
                for s in range(SECTIONS)
            ]
            token = together
            continue
        if c == COMBINE:
            pairs = combine(cross, local, token)
            token = pairs[0]
            continue
        section, state = sections[c], states[c]
        flow = FLOWS[c][section]
        if flow != "p" and not halfway[c]:
            halfway[c] = True
            if flow == "c":
                keep, send = row_step(section, *state, cross, token)
                states[c] = keep, swapped(send, "col", section)
                token = keep
            else:
                own, by_row, by_col, offset = state
                (joined,) = relay_step(section, by_row, by_col, offset, token)
                states[c] = own, by_col, swapped(joined, "row", section), offset
                token = joined
            ended = False
            continue
        weights = (*pairs[2 * section : 2 * section + 2], local, cross, lent[section])
        after = FLOWS[c][section + 1] if section < SECTIONS - 1 else None
        onto = result if after is None else None
        before = None if ended and onto is not None else token
        outs = end_step(section, flow, after, state, weights, before, onto, starts[c], total)
        sections[c], halfway[c] = section + 1, False
        if after is None:
            (result,) = outs
            token, ended = outside(result), True
        else:
            state = sent(after, section + 1, outs)
            states[c] = (*state, 0) if after == "r" else state
            token, ended = outs[0], False
    return result[None, None]


def solution(mesh):
    placed = (
        P("row", "col", None, None, None),
        P("row", "col", None),
        P(None, "row", "col", None, None, None),
        P(None, "row", "col", None, None, None),
    )
    return jax.shard_map(
        shards,
        mesh=mesh,
        in_specs=placed,
        out_specs=P("row", "col", None, None, None),
        check_vma=False,
    )
```

```python
import jax
import jax.numpy as jnp
from jax import lax
from jax.experimental import pallas as pl
from jax.experimental.pallas import tpu as pltpu
from jax.sharding import PartitionSpec as P

SECTIONS = 3
LOCAL = 4
SIZES = (256, 256, 256, 256)
FLOWS = ("rcp", "rpc", "rpp", "rpp")
LATER, COMBINE = -1, -2
ORDER = (0, LATER, 2, COMBINE, 1, 0, 1, 0, 2, 3, 1, 3, 0, 2, 1, 0, 3, 2, 1, 3)
LIMIT = 10 * 2**20

VM = pl.BlockSpec(memory_space=pltpu.VMEM)
ANY = pl.BlockSpec(memory_space=pl.ANY)


def in_vmem(*shape):
    return pltpu.VMEM(shape, jnp.bfloat16)


def held(x):
    return pltpu.with_memory_space_constraint(x, pltpu.VMEM)


def outside(x):
    return pltpu.with_memory_space_constraint(x, pltpu.HBM)


def row_side(section):
    return lax.axis_index("row") >> section & 1


def col_side(section):
    return lax.axis_index("col") >> section & 1


def swapped(piece, axis, section):
    size = lax.axis_size(axis)
    return lax.ppermute(piece, axis, [(i, i ^ 1 << section) for i in range(size)])


def swapped_both(piece, section):
    rows, cols, bit = lax.axis_size("row"), lax.axis_size("col"), 1 << section
    pairs = [(i * cols + j, (i ^ bit) * cols + (j ^ bit)) for i in range(rows) for j in range(cols)]
    return lax.ppermute(piece, ("row", "col"), pairs)


def call(kernel, name, out_shape, operands, token, out_specs=None, scratch=(), result=None):
    operands, specs = list(operands), [ANY if memory == "any" else VM for _, memory in operands]
    operands = [outside(x) if memory == "any" else held(x) for x, memory in operands]
    aliases = {}
    if result is not None:
        aliases = {len(operands): 0}
        operands.append(outside(result))
        specs.append(ANY)
    if token is not None:
        operands.append(token)
        specs.append(ANY)
    extra = len(operands)

    def body(*refs):
        kernel(refs[:extra], refs[extra : extra + len(out_shape)], refs[extra + len(out_shape) :])

    return pl.pallas_call(
        body,
        out_shape=tuple(out_shape),
        in_specs=specs,
        out_specs=(VM,) * len(out_shape) if out_specs is None else out_specs,
        scratch_shapes=list(scratch),
        input_output_aliases=aliases,
        compiler_params=pltpu.CompilerParams(vmem_limit_bytes=LIMIT),
        cost_estimate=pl.CostEstimate(flops=1, bytes_accessed=1, transcendentals=0),
        name=name,
    )(*operands)


def vmem(*arrays):
    return [(x, "vmem") for x in arrays]


def pieces(flow, section):
    row, col = row_side(section), col_side(section)
    if flow == "c":
        return [[(8 * row, 8)], [(8 - 8 * row, 8)]]
    own, by_col, by_row, by_both = [(8 * r + 4 * c, 4) for r in (row, 1 - row) for c in (col, 1 - col)]
    if flow == "p":
        return [[own], [by_row], [by_col], [by_both]]
    return [[own], [by_row], [by_col, by_both]]


COUNTS = {"c": (8, 8), "p": (4, 4, 4, 4), "r": (4, 4, 8)}


def shapes(flow, columns):
    return [in_vmem(count, 64, columns) for count in COUNTS[flow]]


def sent(flow, section, outs):
    if flow == "c":
        return outs[0], swapped(outs[1], "row", section)
    if flow == "p":
        return (
            outs[0],
            swapped(outs[1], "row", section),
            swapped(outs[2], "col", section),
            swapped_both(outs[3], section),
        )
    return outs[0], outs[1], swapped(outs[2], "col", section)


def picked(source, order, start, columns, outs):
    for ranges, out in zip(pieces("r", 0), outs):
        at = 0
        for first, count in ranges:
            for j in range(count):
                out[at] = source[order[0, first + j], :, start : start + columns]
                at += 1


def first_take(order, blocks, columns):
    def kernel(ins, outs, scratch):
        (order_any, source), (order_held, sems) = ins, scratch
        index = pltpu.make_async_copy(order_any, order_held, sems.at[0])
        whole = pltpu.make_async_copy(source, outs[0], sems.at[1])
        whole.start()
        index.start()
        index.wait()
        whole.wait()
        picked(outs[0], order_held, 0, columns, outs[1:])

    return call(
        kernel,
        "take_first",
        [in_vmem(*blocks.shape), *shapes("r", columns)],
        [(order, "any"), (blocks, "any")],
        None,
        scratch=[pltpu.SMEM((1, 16), jnp.int32), pltpu.SemaphoreType.DMA((2,))],
    )


def later_takes(order, blocks, cross, starts, sizes, token):
    total = sum(sizes)

    def kernel(ins, outs, scratch):
        (order_any, source, weights, _), (order_held, sem) = ins, scratch
        index = pltpu.make_async_copy(order_any, order_held, sem)
        index.start()
        for section in range(SECTIONS):
            for p in range(4):
                outs[section][p] = weights[2 * section, 4 - 4 * col_side(section) + p]
        index.wait()
        together = outs[SECTIONS]
        for c, (start, columns) in enumerate(zip(starts, sizes)):
            at = start - starts[0]
            own, by_row = outs[SECTIONS + 1 + 2 * c : SECTIONS + 3 + 2 * c]
            part = together.at[:, :, at : at + columns]
            picked(source, order_held, start, columns, (own, by_row, part))

    outs = call(
        kernel,
        "take_later",
        [in_vmem(4, 128, 128)] * SECTIONS
        + [in_vmem(8, 64, total)]
        + [in_vmem(4, 64, n) for n in sizes for _ in range(2)],
        [(order, "any"), *vmem(blocks, cross)],
        token,
        scratch=[pltpu.SMEM((1, 16), jnp.int32), pltpu.SemaphoreType.DMA],
    )
    return outs[:SECTIONS], outs[SECTIONS], list(zip(outs[SECTIONS + 1 :: 2], outs[SECTIONS + 2 :: 2]))


def combined(first, second, upper, out):
    for j in range(4):
        halves = []
        for g in (j, 4 + j):
            weight = first[g]
            if upper is not None:
                turned = jnp.concatenate([weight[:, 64:], weight[:, :64]], axis=1)
                weight = jnp.where(upper == 1, turned, weight)
            halves.append(weight)
        for t in range(2):
            for i in range(2):
                out[j, 128 * t : 128 * t + 128, 128 * i : 128 * i + 128] = jnp.dot(
                    second[2 * j + t][:, 64 * i : 64 * i + 64],
                    halves[i][64 * t : 64 * t + 64],
                    preferred_element_type=jnp.float32,
                ).astype(jnp.bfloat16)


def combine(cross, local, token):
    def kernel(ins, outs, scratch):
        cross, local = ins[:2]
        for section in range(SECTIONS):
            level, k = 2 * section + 1, section * LOCAL
            combined(cross.at[level], local.at[k], col_side(section), outs[2 * section])
            combined(local.at[k + 1], local.at[k + 2], None, outs[2 * section + 1])

    return call(kernel, "combine", [in_vmem(4, 256, 256)] * (2 * SECTIONS), vmem(cross, local), token)


def times(weight, blocks):
    stacked = jnp.concatenate(blocks, axis=0)
    product = jnp.dot(weight, stacked, preferred_element_type=jnp.float32)
    return product.astype(jnp.bfloat16).reshape(len(blocks), 64, stacked.shape[1])


def paired(weight, upper, own, other):
    return times(weight, [jnp.where(upper == 1, other, own), jnp.where(upper == 1, own, other)])


def row_step(section, keep, arrived, cross, token):
    def kernel(ins, outs, scratch):
        keep, arrived, cross = ins[:3]
        row, col = row_side(section), col_side(section)
        for first, out in ((4 - 4 * col, outs[1]), (4 * col, outs[0])):
            for p in range(4):
                h = first + p
                out[2 * p : 2 * p + 2] = paired(cross[2 * section, h], row, keep[h], arrived[h])

    shape = in_vmem(*keep.shape)
    return call(kernel, f"row_{section}", [shape, shape], vmem(keep, arrived, cross), token)


def relay_step(section, by_row, arrived, offset, token):
    columns = by_row.shape[2]

    def kernel(ins, outs, scratch):
        outs[0][:4] = ins[0][...]
        outs[0][4:] = ins[1][4:, :, offset : offset + columns]

    return call(kernel, f"relay_{section}", [in_vmem(8, 64, columns)], vmem(by_row, arrived), token)


def end_step(section, flow, after, state, weights, token, kept, start, total):
    early, late, local, cross, lent = weights
    columns = state[0].shape[2]
    pieces_in, offset = state, 0
    if flow == "r":
        *pieces_in, offset = state
    operands = vmem(*pieces_in, early, late, local)
    if flow != "c":
        operands += vmem(cross, lent)
    n, m = len(pieces_in), len(operands)
    whole = after is None and sum(part.shape[2] for _, part in kept) + columns == total
    if whole:
        operands += vmem(*(part for _, part in kept))

    def halves(ins, buf):
        if flow == "c":
            return (lambda j: ins[0][j]), (lambda j: ins[1][j])
        own, row, col = ins[0], row_side(section), col_side(section)
        if flow == "p":
            by_row, by_col, by_both = (lambda p: ins[1][p]), (lambda p: ins[2][p]), (lambda p: ins[3][p])
        else:
            by_col = lambda p: ins[1][p, :, offset : offset + columns]
            by_row, by_both = (lambda p: ins[2][p]), (lambda p: ins[2][4 + p])
        cross, lent = ins[n + 3], ins[n + 4]
        for p in range(4):
            buf[1, 2 * p : 2 * p + 2] = paired(cross[2 * section, 4 * col + p], row, own[p], by_row(p))
            buf[1, 8 + 2 * p : 10 + 2 * p] = paired(lent[p], row, by_col(p), by_both(p))
        return (lambda j: buf[1, j]), (lambda j: buf[1, 8 + j])

    def kernel(ins, outs, scratch):
        buf, copies = scratch[0], []
        if whole:
            for i, (at, part) in enumerate(kept):
                there = outs[0].at[:, :, pl.ds(at, part.shape[2])]
                copies.append(pltpu.make_async_copy(ins[m + i], there, scratch[2].at[8 + i]))
            for copy in copies:
                copy.start()
        early, late, local = ins[n : n + 3]
        mine, theirs = halves(ins, buf)
        for j in range(4):
            buf[0, 4 * j : 4 * j + 4] = times(early[j], [mine(j), theirs(j), mine(4 + j), theirs(4 + j)])
        for j in range(4):
            buf[1, 4 * j : 4 * j + 4] = times(late[j], [buf[0, j], buf[0, 8 + j], buf[0, 4 + j], buf[0, 12 + j]])
        last = section * LOCAL + LOCAL - 1

        def final(h):
            return times(local[last, h], [buf[1, h], buf[1, 8 + h]])

        if after is not None:
            for ranges, out in list(zip(pieces(after, section + 1), outs))[::-1]:
                at = 0
                for first, count in ranges:
                    for p in range(count // 2):
                        out[at : at + 2] = final(first // 2 + p)
                        at += 2
            return
        if not whole:
            for h in range(8):
                outs[0][2 * h : 2 * h + 2] = final(h)
            return
        done, sems = scratch[1:]
        for h in range(8):
            done[2 * h : 2 * h + 2] = final(h)
            copy = pltpu.make_async_copy(
                done.at[pl.ds(2 * h, 2)],
                outs[0].at[pl.ds(2 * h, 2), :, pl.ds(start, columns)],
                sems.at[h],
            )
            copy.start()
            copies.append(copy)
        for copy in copies:
            copy.wait()

    scratch = [in_vmem(2, 16, 64, columns)]
    if after is not None:
        return call(
            kernel, f"end_{section}", shapes(after, columns), operands, token, scratch=scratch
        )
    if not whole:
        shape = [in_vmem(16, 64, columns)]
        return call(kernel, f"end_{section}", shape, operands, token, scratch=scratch)
    scratch += [in_vmem(16, 64, columns), pltpu.SemaphoreType.DMA((8 + len(kept),))]
    return call(
        kernel,
        f"end_{section}",
        [pltpu.HBM((16, 64, total), jnp.bfloat16)],
        operands,
        token,
        out_specs=(ANY,),
        scratch=scratch,
    )


def shards(blocks, order, cross_weights, local_weights):
    blocks, order = blocks[0, 0], order[0]
    cross, local = cross_weights[:, 0, 0], local_weights[:, 0, 0]
    total = blocks.shape[2]
    starts = [sum(SIZES[:c]) for c in range(len(SIZES))]
    blocks, *outs = first_take(order, blocks, SIZES[0])
    states = {0: (*sent("r", 0, outs), 0)}
    token, kept = outs[0], []
    sections, halfway = [0] * len(SIZES), [False] * len(SIZES)
    for c in ORDER:
        if c == LATER:
            lend, together, rest = later_takes(order, blocks, cross, starts[1:], SIZES[1:], token)
            arrived = swapped(together, "col", 0)
            for k, pair in enumerate(rest, 1):
                states[k] = (*pair, arrived, starts[k] - starts[1])
            lent = [
                swapped(lend[s], "col", s) if any(flows[s] != "c" for flows in FLOWS) else None
                for s in range(SECTIONS)
            ]
            token = together
            continue
        if c == COMBINE:
            pairs = combine(cross, local, token)
            token = pairs[0]
            continue
        section, state = sections[c], states[c]
        flow = FLOWS[c][section]
        if flow != "p" and not halfway[c]:
            halfway[c] = True
            if flow == "c":
                keep, send = row_step(section, *state, cross, token)
                states[c] = keep, swapped(send, "col", section)
                token = keep
            else:
                own, by_row, by_col, offset = state
                (joined,) = relay_step(section, by_row, by_col, offset, token)
                states[c] = own, by_col, swapped(joined, "row", section), offset
                token = joined
            continue
        weights = (*pairs[2 * section : 2 * section + 2], local, cross, lent[section])
        after = FLOWS[c][section + 1] if section < SECTIONS - 1 else None
        outs = end_step(section, flow, after, state, weights, token, kept, starts[c], total)
        sections[c], halfway[c] = section + 1, False
        token = outs[0]
        if after is None:
            kept.append((starts[c], token))
        else:
            state = sent(after, section + 1, outs)
            states[c] = (*state, 0) if after == "r" else state
    return token[None, None]


def solution(mesh):
    placed = (
        P("row", "col", None, None, None),
        P("row", "col", None),
        P(None, "row", "col", None, None, None),
        P(None, "row", "col", None, None, None),
    )
    return jax.shard_map(
        shards,
        mesh=mesh,
        in_specs=placed,
        out_specs=P("row", "col", None, None, None),
        check_vma=False,
    )
```
